1024 devices in a mesh: lgroup: 8 (over z_hi, core), row: 128 (over x, y, z_lo).
Axes of the slice: x: 4, y: 8, z: 16 (z_hi: 4, z_lo: 4; z = z_hi * 4 + z_lo), core: 2. Of those that a mesh axis runs over, the one named last changes fastest.
Arguments:
- psi_in: float32 [2, 512, 1024, 128], P(None, 'lgroup', 'row'), may hold values from -6 to 6
- channels: int32 [8, 2, 64], P('lgroup'), may hold values from -1 to 11, as said below
- multipole: float32 [8, 3, 64, 64], P('lgroup'), may hold values from -0.18 to 0.18
- dipole: float32 [8, 2, 64, 64], P('lgroup'), may hold values from -0.36 to 0.36
Outputs:
- psi_out: float32 [2, 512, 1024, 128], P(None, 'lgroup', 'row')
The draws below stay inside these ranges and needn't reach their ends.
Inputs may be any that keep to these rules, and one draw needn't show every extreme that they name: In each block the live channels fill the first slots and hold l1 and l2 of 0 to 11; the other slots hold -1 in both entries. Each block has 64 / 4 (rounded down) or more live slots, and some block has all 64 live.
All inputs are finite; a program needn't handle non-finite values.
Results may differ from the reference program's by a relative error of at most 0.0001.
Values sent between devices are 32-bit elements; how exact they have to be, the bound alone decides.
No kernel may reach another device: no remote copies, remote signals or barrier semaphores. Data moves between devices by JAX's collectives and lax.ppermute only.
A program may use at most 32 MiB of HBM per device.

```python
import jax
import jax.numpy as jnp
from jax import lax

CPG = 64
LAM = 3
ORDER = 4
LMAX = 11
R2 = 128
NG = 8
CHAN = 512
R1 = 1024


def draw_channels(key, part):
    key_count, key_full, key_values = jax.random.split(key, 3)
    counts = jax.random.randint(key_count, (NG,), CPG // 4, CPG + 1)
    full_group = jax.random.randint(key_full, (), 0, NG)
    counts = jnp.where(jnp.arange(NG) == full_group, CPG, counts)
    values = jax.random.randint(key_values, (NG, 2, CPG), 0, LMAX + 1)
    live_slots = jnp.arange(CPG)[None, :] < counts[:, None]
    return jnp.where(live_slots[:, None, :], values, -1).astype(jnp.int32)


def steps_of(key, extent, shards, smallest, top_value):
    factor_of, own = 1.0, jax.random.fold_in(key, 6)
    for axis_at, blocks in shards:
        heights = jnp.exp(jax.random.uniform(jax.random.fold_in(own, axis_at), (blocks,), jnp.float32, smallest / len(shards), top_value / len(shards)))
        factor_of = factor_of * jnp.repeat(heights, extent[axis_at] // blocks).reshape([-1 if axis == axis_at else 1 for axis in range(len(extent))])
    return factor_of


def centred(stream_key, extent, scale, reach, cuts=(), held_as=jnp.bfloat16):
    array = jax.random.normal(stream_key, extent, jnp.float32) * scale
    if len(cuts) > 0:
        array = steps_of(stream_key, extent, cuts, -0.22, 0.18) * array
    return jnp.clip(array, min=-reach, max=reach).astype(held_as)


def setup_inputs(seed: int = 0) -> dict:
    key_list = jax.random.split(jax.random.key(seed), 5)
    psi_in = centred(key_list[0], (2, CHAN, R1, R2), 1.0, 6.0, ((1, 8), (2, 128)), jnp.float32)
    channels = draw_channels(jax.random.fold_in(key_list[4], 71), 0)
    multipole = centred(key_list[2], (NG, LAM, CPG, CPG), 0.03, 0.18, ((0, 8),), jnp.float32)
    dipole = centred(key_list[3], (NG, 2, CPG, CPG), 0.06, 0.36, ((0, 8),), jnp.float32)
    return {"psi_in": psi_in, "channels": channels, "multipole": multipole, "dipole": dipole}


kinetic_scale = 0.2
coulomb_charge = 4.0
radius_offset = 16.0
center_weight = -2.5
near_weight = 4.0 / 3.0
far_weight = -1.0 / 12.0


def reference(psi_in, channels, multipole, dipole):
    groups = channels.shape[0]
    slots = channels.shape[2]
    rows_one = psi_in.shape[2]
    rows_two = psi_in.shape[3]
    live_mask = (channels[:, 0, :] >= 0).astype(jnp.float32)
    ang_one = channels[:, 0, :].astype(jnp.float32)
    ang_two = channels[:, 1, :].astype(jnp.float32)
    radius_one = jnp.arange(rows_one).astype(jnp.float32) + radius_offset
    radius_two = jnp.arange(rows_two).astype(jnp.float32) + radius_offset
    potential = ((ang_one * (ang_one + 1.0))[:, :, None, None] / (radius_one ** 2)[:, None]
                 + (ang_two * (ang_two + 1.0))[:, :, None, None] / (radius_two ** 2)[None, :]
                 - coulomb_charge * (1.0 / radius_one[:, None] + 1.0 / radius_two[None, :]))
    radius_ratio = (jnp.minimum(radius_one[:, None], radius_two[None, :])
                    / jnp.maximum(radius_one[:, None], radius_two[None, :]))
    coupling = 0.5 * (multipole + jnp.swapaxes(multipole, -1, -2))
    weight_one = (radius_one / (rows_one + radius_offset))[:, None]
    weight_two = (radius_two / (rows_two + radius_offset))[None, :]
    mat_a = dipole[:, 0]
    mat_b = dipole[:, 1]
    zero_mat = jnp.zeros_like(mat_a[:1])
    prev_a = jnp.concatenate([zero_mat, mat_a[:-1]], axis=0)
    prev_b = jnp.concatenate([zero_mat, mat_b[:-1]], axis=0)
    highest = lax.Precision.HIGHEST

    def apply_operator(field):
        padded = jnp.pad(field, ((0, 0), (0, 0), (0, 0), (2, 2), (2, 2)))
        laplace = 2.0 * center_weight * field
        laplace = laplace + near_weight * (padded[..., 3:-1, 2:-2] + padded[..., 1:-3, 2:-2]
                                           + padded[..., 2:-2, 3:-1] + padded[..., 2:-2, 1:-3])
        laplace = laplace + far_weight * (padded[..., 4:, 2:-2] + padded[..., :-4, 2:-2]
                                          + padded[..., 2:-2, 4:] + padded[..., 2:-2, :-4])
        result = -kinetic_scale * laplace + potential * field
        for degree in range(coupling.shape[1]):
            result = result + (radius_ratio ** degree) * jnp.einsum(
                'gcd,sgdij->sgcij', coupling[:, degree], field, precision=highest)
        zero_block = jnp.zeros_like(field[:, :1])
        upper = jnp.concatenate([field[:, 1:], zero_block], axis=1)
        lower = jnp.concatenate([zero_block, field[:, :-1]], axis=1)
        part_one = (jnp.einsum('gcd,sgdij->sgcij', mat_a, upper, precision=highest)
                    + jnp.einsum('gdc,sgdij->sgcij', prev_a, lower, precision=highest))
        part_two = (jnp.einsum('gcd,sgdij->sgcij', mat_b, upper, precision=highest)
                    + jnp.einsum('gdc,sgdij->sgcij', prev_b, lower, precision=highest))
        result = result + weight_one * part_one + weight_two * part_two
        return result * live_mask[None, :, :, None, None]

    start = psi_in.reshape(2, groups, slots, rows_one, rows_two) * live_mask[None, :, :, None, None]
    total = start
    term = start
    for order_index in range(1, ORDER + 1):
        image = apply_operator(term)
        term = jnp.stack([image[1], -image[0]]) / float(order_index)
        total = total + term
    return total.reshape(2, groups * slots, rows_one, rows_two)
```

```python
import functools

import jax
import jax.numpy as jnp
from jax import lax
from jax.experimental import pallas as pl
from jax.experimental.pallas import tpu as pltpu
from jax.sharding import PartitionSpec as P

ORDER = 4

kinetic_scale = 0.2
coulomb_charge = 4.0
radius_offset = 16.0
center_weight = -2.5
near_weight = 4.0 / 3.0
far_weight = -1.0 / 12.0

near = -kinetic_scale * near_weight
far = -kinetic_scale * far_weight

f32 = jnp.float32
bf16 = jnp.bfloat16


def split_weights(mat):
    rounded = lax.reduce_precision(mat, 8, 7)
    high = rounded.astype(bf16)
    low = (mat - rounded).astype(bf16)
    return jnp.concatenate([high, high, low], axis=1)


def split_field(x):
    high = x.astype(bf16)
    low = (x - high.astype(f32)).astype(bf16)
    return jnp.concatenate([high, low, high], axis=0)


def both(ref, i):
    return jnp.concatenate([ref[0, i], ref[1, i]], axis=1)


def times(weights, x):
    return jnp.dot(weights, split_field(x), preferred_element_type=f32)


def twice(row):
    return jnp.concatenate([row, row], axis=1)


def start_kernel(psi_ref, live_ref, term_ref):
    live = live_ref[...]
    for s in range(2):
        for i in range(term_ref.shape[1]):
            term_ref[s, i] = psi_ref[s, :, i, :] * live


def own_kernel(term_ref, weights_ref, coef_ref, pot_ref, out_ref, low_ref, high_ref):
    rows = term_ref.shape[1]
    slots = term_ref.shape[2]
    lanes = term_ref.shape[3]
    low_ref[...] = term_ref[:, 0:2]
    high_ref[...] = term_ref[:, rows - 2 : rows]
    lane = lax.broadcasted_iota(jnp.int32, (slots, lanes), 1)
    weights = weights_ref[...]
    for i in range(rows):
        mixed = times(weights, both(term_ref, i))
        ratio = twice(coef_ref[i, 0:1])
        mixed = mixed[:slots] + ratio * (mixed[slots : 2 * slots] + ratio * mixed[2 * slots :])
        for s in range(2):
            x = term_ref[s, i]
            acc = mixed[:, s * lanes : (s + 1) * lanes] + pot_ref[i] * x
            close = jnp.where(lane >= 1, pltpu.roll(x, 1, 1), 0.0) + jnp.where(
                lane < lanes - 1, pltpu.roll(x, lanes - 1, 1), 0.0
            )
            wide = jnp.where(lane >= 2, pltpu.roll(x, 2, 1), 0.0) + jnp.where(
                lane < lanes - 2, pltpu.roll(x, lanes - 2, 1), 0.0
            )
            for step in (-1, 1):
                if 0 <= i + step < rows:
                    close = close + term_ref[s, i + step]
                if 0 <= i + 2 * step < rows:
                    wide = wide + term_ref[s, i + 2 * step]
            out_ref[s, i] = acc + near * close + far * wide


def chip_kernel(part_ref, other_ref, weights_ref, coef_ref, below_ref, above_ref, out_ref):
    rows, slots, lanes = out_ref.shape[1:]
    weights = weights_ref[...]
    for i in range(rows):
        mixed = times(weights, both(other_ref, i))
        mixed = twice(coef_ref[i, 1:2]) * mixed[:slots] + twice(coef_ref[i, 2:3]) * mixed[slots:]
        for s in range(2):
            acc = part_ref[s, i] + mixed[:, s * lanes : (s + 1) * lanes]
            if i == 0:
                acc = acc + near * below_ref[s, 1] + far * below_ref[s, 0]
            if i == 1:
                acc = acc + far * below_ref[s, 1]
            if i == rows - 1:
                acc = acc + near * above_ref[s, 0] + far * above_ref[s, 1]
            if i == rows - 2:
                acc = acc + far * above_ref[s, 0]
            out_ref[s, i] = acc


def finish_kernel(order_index, last, part_ref, other_ref, weights_ref, coef_ref, live_ref, total_ref, *outs):
    rows, slots, lanes = part_ref.shape[1:]
    weights = weights_ref[...]
    scale = live_ref[...] / float(order_index)
    for i in range(rows):
        mixed = times(weights, both(other_ref, i))
        mixed = twice(coef_ref[i, 1:2]) * mixed[:slots] + twice(coef_ref[i, 2:3]) * mixed[slots:]
        real = (part_ref[1, i] + mixed[:, lanes:]) * scale
        imag = -((part_ref[0, i] + mixed[:, :lanes]) * scale)
        if last:
            outs[0][0, :, i, :] = total_ref[0, i] + real
            outs[0][1, :, i, :] = total_ref[1, i] + imag
        else:
            outs[0][0, i] = real
            outs[0][1, i] = imag
            outs[1][0, i] = total_ref[0, i] + real
            outs[1][1, i] = total_ref[1, i] + imag


def call(kernel, outs, *args):
    cost = pl.CostEstimate(flops=800_000_000, bytes_accessed=3_000_000, transcendentals=0)
    return pl.pallas_call(
        kernel,
        out_shape=outs,
        cost_estimate=cost,
        compiler_params=pltpu.CompilerParams(vmem_limit_bytes=32 * 1024 * 1024),
    )(*args)


def swaps(count, first):
    found = []
    for i in range(first, count - 1, 2):
        found += [(i, i + 1), (i + 1, i)]
    return found


def shifts(count, by):
    return [(i, i + by) for i in range(count) if 0 <= i + by < count]


def local(psi_in, channels, multipole, dipole):
    _, slots, rows, lanes = psi_in.shape
    blocks = lax.axis_size("lgroup")
    strips = lax.axis_size("row")
    total_rows = strips * rows
    first_row = lax.axis_index("row") * rows
    even = lax.axis_index("lgroup") % 2 == 0

    field = jax.ShapeDtypeStruct((2, rows, slots, lanes), f32)
    edge = jax.ShapeDtypeStruct((2, 2, slots, lanes), f32)
    live = (channels[0, 0, :] >= 0).astype(f32)[:, None]
    live = jnp.broadcast_to(live, (slots, lanes))
    term = call(start_kernel, field, psi_in, live)

    ang_one = channels[0, 0, :].astype(f32)
    ang_two = channels[0, 1, :].astype(f32)
    radius_one = (first_row + jnp.arange(rows)).astype(f32) + radius_offset
    radius_two = jnp.arange(lanes).astype(f32) + radius_offset
    potential = (
        (ang_one * (ang_one + 1.0))[None, :, None] / (radius_one**2)[:, None, None]
        + (ang_two * (ang_two + 1.0))[None, :, None] / (radius_two**2)[None, None, :]
        - coulomb_charge * (1.0 / radius_one[:, None, None] + 1.0 / radius_two[None, None, :])
    ) - kinetic_scale * 2.0 * center_weight
    ratio = jnp.minimum(radius_one[:, None], radius_two[None, :]) / jnp.maximum(
        radius_one[:, None], radius_two[None, :]
    )
    weight_one = jnp.broadcast_to((radius_one / (total_rows + radius_offset))[:, None], (rows, lanes))
    weight_two = jnp.broadcast_to((radius_two / (lanes + radius_offset))[None, :], (rows, lanes))
    coef = jnp.stack([ratio, weight_one, weight_two] + [jnp.zeros_like(ratio)] * 5, axis=1)

    coupling = 0.5 * (multipole[0] + jnp.swapaxes(multipole[0], -1, -2))
    own = split_weights(coupling.reshape(-1, slots))
    lower = lax.ppermute(dipole[0], "lgroup", shifts(blocks, 1))
    upward = dipole[0].reshape(-1, slots)
    downward = jnp.swapaxes(lower, -1, -2).reshape(-1, slots)
    chip_weights = split_weights(jnp.where(even, upward, downward))
    cross_weights = split_weights(jnp.where(even, downward, upward))

    total = term
    for order_index in range(1, ORDER + 1):
        across = lax.ppermute(term, "lgroup", swaps(blocks, 1))
        beside = lax.ppermute(term, "lgroup", swaps(blocks, 0))
        part, low, high = call(own_kernel, (field, edge, edge), term, own, coef, potential)
        below = lax.ppermute(high, "row", shifts(strips, 1))
        above = lax.ppermute(low, "row", shifts(strips, -1))
        part = call(chip_kernel, field, part, beside, chip_weights, coef, below, above)
        last = order_index == ORDER
        outs = jax.ShapeDtypeStruct(psi_in.shape, f32) if last else (field, field)
        done = call(
            functools.partial(finish_kernel, order_index, last),
            outs, part, across, cross_weights, coef, live, total,
        )
        if last:
            return done
        term, total = done


def solution(mesh):
    placed = (
        P(None, "lgroup", "row", None),
        P("lgroup", None, None),
        P("lgroup", None, None, None),
        P("lgroup", None, None, None),
    )
    return jax.shard_map(
        local, mesh=mesh, in_specs=placed, out_specs=P(None, "lgroup", "row", None), check_vma=False
    )
```

```python
import functools

import jax
import jax.numpy as jnp
from jax import lax
from jax.experimental import pallas as pl
from jax.experimental.pallas import tpu as pltpu
from jax.sharding import PartitionSpec as P

ORDER = 4

kinetic_scale = 0.2
coulomb_charge = 4.0
radius_offset = 16.0
center_weight = -2.5
near_weight = 4.0 / 3.0
far_weight = -1.0 / 12.0

near = -kinetic_scale * near_weight
far = -kinetic_scale * far_weight

f32 = jnp.float32
bf16 = jnp.bfloat16


def split_weights(mat):
    rounded = lax.reduce_precision(mat, 8, 7)
    high = rounded.astype(bf16)
    low = (mat - rounded).astype(bf16)
    return jnp.concatenate([high, high, low], axis=1)


def split_field(x):
    high = x.astype(bf16)
    low = (x - high.astype(f32)).astype(bf16)
    return jnp.concatenate([high, low, high], axis=0)


def both(ref, i):
    return jnp.concatenate([ref[0, i], ref[1, i]], axis=1)


def times(weights, x):
    return jnp.dot(weights, split_field(x), preferred_element_type=f32)


def twice(row):
    return jnp.concatenate([row, row], axis=1)


def start_kernel(psi_ref, live_ref, term_ref, low_ref, high_ref):
    live = live_ref[...]
    rows = term_ref.shape[1]
    for s in range(2):
        for i in range(rows):
            term_ref[s, i] = psi_ref[s, :, i, :] * live
    low_ref[...] = term_ref[:, 0:2]
    high_ref[...] = term_ref[:, rows - 2 : rows]


def own_kernel(term_ref, weights_ref, sent_ref, coef_ref, pot_ref, out_ref, copy_ref, message_ref):
    copy_ref[...] = term_ref[...]
    kept = message_ref.shape[2]
    rows = term_ref.shape[1]
    slots = term_ref.shape[2]
    lanes = term_ref.shape[3]
    lane = lax.broadcasted_iota(jnp.int32, (slots, lanes), 1)
    weights = weights_ref[...]
    for i in range(rows):
        here = both(term_ref, i)
        sent = times(sent_ref[...], here)
        sent = twice(coef_ref[i, 1:2]) * sent[:kept] + twice(coef_ref[i, 2:3]) * sent[slots : slots + kept]
        sent = twice(coef_ref[i, 3:4]) * here[:kept] + twice(coef_ref[i, 4:5]) * sent
        for s in range(2):
            message_ref[s, i] = sent[:, s * lanes : (s + 1) * lanes]
        mixed = times(weights, here)
        ratio = twice(coef_ref[i, 0:1])
        mixed = mixed[:slots] + ratio * (mixed[slots : 2 * slots] + ratio * mixed[2 * slots :])
        for s in range(2):
            x = term_ref[s, i]
            acc = mixed[:, s * lanes : (s + 1) * lanes] + pot_ref[i] * x
            close = jnp.where(lane >= 1, pltpu.roll(x, 1, 1), 0.0) + jnp.where(
                lane < lanes - 1, pltpu.roll(x, lanes - 1, 1), 0.0
            )
            wide = jnp.where(lane >= 2, pltpu.roll(x, 2, 1), 0.0) + jnp.where(
                lane < lanes - 2, pltpu.roll(x, lanes - 2, 1), 0.0
            )
            for step in (-1, 1):
                if 0 <= i + step < rows:
                    close = close + term_ref[s, i + step]
                if 0 <= i + 2 * step < rows:
                    wide = wide + term_ref[s, i + 2 * step]
            out_ref[s, i] = acc + near * close + far * wide


def finish_kernel(
    order_index, last, part_ref, across_ref, beside_ref, below_ref, above_ref,
    cross_ref, chip_ref, coef_ref, live_ref, total_ref, *outs
):
    rows, slots, lanes = part_ref.shape[1:]
    kept = across_ref.shape[2]
    scale = live_ref[...] / float(order_index)
    for i in range(rows):
        came = both(across_ref, i)
        if kept < slots:
            came = jnp.concatenate([came, jnp.zeros((slots - kept, 2 * lanes), f32)], axis=0)
        raw = came * twice(coef_ref[i, 4:5])
        mixed = times(cross_ref[...], raw) + times(chip_ref[...], both(beside_ref, i))
        mixed = twice(coef_ref[i, 1:2]) * mixed[:slots] + twice(coef_ref[i, 2:3]) * mixed[slots:]
        mixed = mixed + came * twice(coef_ref[i, 3:4])
        image = []
        for s in range(2):
            acc = part_ref[s, i] + mixed[:, s * lanes : (s + 1) * lanes]
            if i == 0:
                acc = acc + near * below_ref[s, 1] + far * below_ref[s, 0]
            if i == 1:
                acc = acc + far * below_ref[s, 1]
            if i == rows - 1:
                acc = acc + near * above_ref[s, 0] + far * above_ref[s, 1]
            if i == rows - 2:
                acc = acc + far * above_ref[s, 0]
            image.append(acc * scale)
        real, imag = image[1], -image[0]
        if last:
            outs[0][0, :, i, :] = total_ref[0, i] + real
            outs[0][1, :, i, :] = total_ref[1, i] + imag
            continue
        for s, value in enumerate((real, imag)):
            outs[0][s, i] = value
            outs[1][s, i] = total_ref[s, i] + value
            if i < 2:
                outs[2][s, i] = value
            if i >= rows - 2:
                outs[3][s, i - (rows - 2)] = value


def call(kernel, outs, *args):
    cost = pl.CostEstimate(flops=800_000_000, bytes_accessed=3_000_000, transcendentals=0)
    return pl.pallas_call(
        kernel,
        out_shape=outs,
        cost_estimate=cost,
        compiler_params=pltpu.CompilerParams(vmem_limit_bytes=32 * 1024 * 1024),
    )(*args)


def swaps(count, first):
    found = []
    for i in range(first, count - 1, 2):
        found += [(i, i + 1), (i + 1, i)]
    return found


def shifts(count, by):
    return [(i, i + by) for i in range(count) if 0 <= i + by < count]


def local(psi_in, channels, multipole, dipole):
    _, slots, rows, lanes = psi_in.shape
    blocks = lax.axis_size("lgroup")
    strips = lax.axis_size("row")
    total_rows = strips * rows
    first_row = lax.axis_index("row") * rows
    even = lax.axis_index("lgroup") % 2 == 0

    field = jax.ShapeDtypeStruct((2, rows, slots, lanes), f32)
    edge = jax.ShapeDtypeStruct((2, 2, slots, lanes), f32)
    live = (channels[0, 0, :] >= 0).astype(f32)[:, None]
    live = jnp.broadcast_to(live, (slots, lanes))
    term, low, high = call(start_kernel, (field, edge, edge), psi_in, live)

    ang_one = channels[0, 0, :].astype(f32)
    ang_two = channels[0, 1, :].astype(f32)
    radius_one = (first_row + jnp.arange(rows)).astype(f32) + radius_offset
    radius_two = jnp.arange(lanes).astype(f32) + radius_offset
    potential = (
        (ang_one * (ang_one + 1.0))[None, :, None] / (radius_one**2)[:, None, None]
        + (ang_two * (ang_two + 1.0))[None, :, None] / (radius_two**2)[None, None, :]
        - coulomb_charge * (1.0 / radius_one[:, None, None] + 1.0 / radius_two[None, None, :])
    ) - kinetic_scale * 2.0 * center_weight
    ratio = jnp.minimum(radius_one[:, None], radius_two[None, :]) / jnp.maximum(
        radius_one[:, None], radius_two[None, :]
    )
    weight_one = jnp.broadcast_to((radius_one / (total_rows + radius_offset))[:, None], (rows, lanes))
    weight_two = jnp.broadcast_to((radius_two / (lanes + radius_offset))[None, :], (rows, lanes))

    alive = jnp.sum(channels[0, 0, :] >= 0).astype(f32)
    counts = lax.all_to_all(jnp.full((blocks, 8, 128), alive), "lgroup", 0, 0)[:, 0, 0]
    most = jnp.max(jnp.minimum(counts[1 : blocks - 1 : 2], counts[2:blocks:2])).astype(jnp.int32)
    place = lax.axis_index("lgroup")
    facing = jnp.clip(jnp.where(even, place - 1, place + 1), 0, blocks - 1)
    theirs = jnp.sum(jnp.where(jnp.arange(blocks) == facing, counts, 0.0))
    fewer = jnp.where(even, alive < theirs, alive <= theirs)

    def coefficients(small):
        small = jnp.broadcast_to(small.astype(f32), (rows, lanes))
        spare = [jnp.zeros_like(ratio)] * 3
        return jnp.stack([ratio, weight_one, weight_two, small, 1.0 - small] + spare, axis=1)

    coupling = 0.5 * (multipole[0] + jnp.swapaxes(multipole[0], -1, -2))
    own = split_weights(coupling.reshape(-1, slots))
    lower = lax.ppermute(dipole[0], "lgroup", shifts(blocks, 1))
    upward = dipole[0].reshape(-1, slots)
    downward = jnp.swapaxes(lower, -1, -2).reshape(-1, slots)
    chip_weights = split_weights(jnp.where(even, upward, downward))
    cross_weights = split_weights(jnp.where(even, downward, upward))
    onward = jnp.swapaxes(dipole[0], -1, -2).reshape(-1, slots)
    sent_weights = split_weights(jnp.where(even, lower.reshape(-1, slots), onward))

    def apply(order_index, coef, roles, sent_by, kept, state):
        term, total, low, high = state
        message = jax.ShapeDtypeStruct((2, rows, kept, lanes), f32)
        part, copied, message = call(
            own_kernel, (field, field, message), term, own, sent_by, coef, potential
        )
        across = lax.ppermute(message, "lgroup", swaps(blocks, 1))
        beside = lax.ppermute(copied, "lgroup", swaps(blocks, 0))
        below = lax.ppermute(high, "row", shifts(strips, 1))
        above = lax.ppermute(low, "row", shifts(strips, -1))
        last = order_index == ORDER
        outs = jax.ShapeDtypeStruct(psi_in.shape, f32) if last else (field, field, edge, edge)
        return call(
            functools.partial(finish_kernel, order_index, last),
            outs, part, across, beside, below, above, cross_weights, chip_weights, roles, live, total,
        )

    def rest(kept):
        def run(roles, state):
            for order_index in range(2, ORDER + 1):
                state = apply(order_index, roles, roles, sent_weights, kept, state)
            return state

        return run

    everyone = jnp.bool_(True)
    first = (term, term, low, high)
    state = apply(1, coefficients(everyone), coefficients(~everyone), own[: 2 * slots], slots, first)
    sizes = list(range(24, slots, 8)) + [slots]
    chosen = jnp.sum(most > jnp.asarray(sizes[:-1], jnp.int32)).astype(jnp.int32)
    return lax.switch(chosen, [rest(kept) for kept in sizes], coefficients(fewer), state)


def solution(mesh):
    placed = (
        P(None, "lgroup", "row", None),
        P("lgroup", None, None),
        P("lgroup", None, None, None),
        P("lgroup", None, None, None),
    )
    return jax.shard_map(
        local, mesh=mesh, in_specs=placed, out_specs=P(None, "lgroup", "row", None), check_vma=False
    )
```

```python
import functools

import jax
import jax.numpy as jnp
from jax import lax
from jax.experimental import pallas as pl
from jax.experimental.pallas import tpu as pltpu
from jax.sharding import PartitionSpec as P

ORDER = 4

kinetic_scale = 0.2
coulomb_charge = 4.0
radius_offset = 16.0
center_weight = -2.5
near_weight = 4.0 / 3.0
far_weight = -1.0 / 12.0

near = -kinetic_scale * near_weight
far = -kinetic_scale * far_weight

f32 = jnp.float32
bf16 = jnp.bfloat16


def split_weights(mat):
    rounded = lax.reduce_precision(mat, 8, 7)
    high = rounded.astype(bf16)
    low = (mat - rounded).astype(bf16)
    return jnp.concatenate([high, high, low], axis=1)


def split_field(x):
    high = x.astype(bf16)
    low = (x - high.astype(f32)).astype(bf16)
    return jnp.concatenate([high, low, high], axis=0)


def both(ref, i):
    return jnp.concatenate([ref[0, i], ref[1, i]], axis=1)


def times(weights, x):
    return jnp.dot(weights, split_field(x), preferred_element_type=f32)


def twice(row):
    return jnp.concatenate([row, row], axis=1)


def start_kernel(psi_ref, live_ref, dipole_ref, term_ref, low_ref, high_ref, sent_ref):
    sent_ref[...] = dipole_ref[...]
    live = live_ref[...]
    rows = term_ref.shape[1]
    for s in range(2):
        for i in range(rows):
            term_ref[s, i] = psi_ref[s, :, i, :] * live
    low_ref[...] = term_ref[:, 0:2]
    high_ref[...] = term_ref[:, rows - 2 : rows]


def own_kernel(sends, term_ref, weights_ref, coef_ref, pot_ref, *refs):
    if sends:
        sent_ref, out_ref, copy_ref, message_ref = refs
        copy_ref[...] = term_ref[...]
        kept = message_ref.shape[2]
    else:
        (out_ref,) = refs
    rows, slots, lanes = term_ref.shape[1:]
    lane = lax.broadcasted_iota(jnp.int32, (slots, lanes), 1)
    weights = weights_ref[...]
    for i in range(rows):
        here = both(term_ref, i)
        if sends:
            sent = times(sent_ref[...], here)
            sent = twice(coef_ref[i, 1:2]) * sent[:kept] + twice(coef_ref[i, 2:3]) * sent[slots : slots + kept]
            sent = twice(coef_ref[i, 3:4]) * here[:kept] + twice(coef_ref[i, 4:5]) * sent
            for s in range(2):
                message_ref[s, i] = sent[:, s * lanes : (s + 1) * lanes]
        mixed = times(weights, here)
        ratio = twice(coef_ref[i, 0:1])
        mixed = mixed[:slots] + ratio * (mixed[slots : 2 * slots] + ratio * mixed[2 * slots :])
        for s in range(2):
            x = term_ref[s, i]
            acc = mixed[:, s * lanes : (s + 1) * lanes] + pot_ref[i] * x
            close = jnp.where(lane >= 1, pltpu.roll(x, 1, 1), 0.0) + jnp.where(
                lane < lanes - 1, pltpu.roll(x, lanes - 1, 1), 0.0
            )
            wide = jnp.where(lane >= 2, pltpu.roll(x, 2, 1), 0.0) + jnp.where(
                lane < lanes - 2, pltpu.roll(x, lanes - 2, 1), 0.0
            )
            for step in (-1, 1):
                if 0 <= i + step < rows:
                    close = close + term_ref[s, i + step]
                if 0 <= i + 2 * step < rows:
                    wide = wide + term_ref[s, i + 2 * step]
            out_ref[s, i] = acc + near * close + far * wide


def finish_kernel(
    order_index, last, part_ref, across_ref, beside_ref, below_ref, above_ref,
    cross_ref, chip_ref, coef_ref, live_ref, total_ref, *outs
):
    rows, slots, lanes = part_ref.shape[1:]
    kept = across_ref.shape[2]
    scale = live_ref[...] / float(order_index)
    for i in range(rows):
        came = both(across_ref, i)
        if kept < slots:
            came = jnp.concatenate([came, jnp.zeros((slots - kept, 2 * lanes), f32)], axis=0)
        raw = came * twice(coef_ref[i, 4:5])
        mixed = times(cross_ref[...], raw) + times(chip_ref[...], both(beside_ref, i))
        mixed = twice(coef_ref[i, 1:2]) * mixed[:slots] + twice(coef_ref[i, 2:3]) * mixed[slots:]
        mixed = mixed + came * twice(coef_ref[i, 3:4])
        image = []
        for s in range(2):
            acc = part_ref[s, i] + mixed[:, s * lanes : (s + 1) * lanes]
            if i == 0:
                acc = acc + near * below_ref[s, 1] + far * below_ref[s, 0]
            if i == 1:
                acc = acc + far * below_ref[s, 1]
            if i == rows - 1:
                acc = acc + near * above_ref[s, 0] + far * above_ref[s, 1]
            if i == rows - 2:
                acc = acc + far * above_ref[s, 0]
            image.append(acc * scale)
        real, imag = image[1], -image[0]
        if last:
            outs[0][0, :, i, :] = total_ref[0, i] + real
            outs[0][1, :, i, :] = total_ref[1, i] + imag
            continue
        for s, value in enumerate((real, imag)):
            outs[0][s, i] = value
            outs[1][s, i] = total_ref[s, i] + value
            if i < 2:
                outs[2][s, i] = value
            if i >= rows - 2:
                outs[3][s, i - (rows - 2)] = value


def call(kernel, outs, *args):
    cost = pl.CostEstimate(flops=800_000_000, bytes_accessed=3_000_000, transcendentals=0)
    return pl.pallas_call(
        kernel,
        out_shape=outs,
        cost_estimate=cost,
        compiler_params=pltpu.CompilerParams(vmem_limit_bytes=32 * 1024 * 1024),
    )(*args)


def swaps(count, first):
    found = []
    for i in range(first, count - 1, 2):
        found += [(i, i + 1), (i + 1, i)]
    return found


def shifts(count, by):
    return [(i, i + by) for i in range(count) if 0 <= i + by < count]


def local(psi_in, channels, multipole, dipole):
    _, slots, rows, lanes = psi_in.shape
    blocks = lax.axis_size("lgroup")
    strips = lax.axis_size("row")
    total_rows = strips * rows
    first_row = lax.axis_index("row") * rows
    even = lax.axis_index("lgroup") % 2 == 0

    field = jax.ShapeDtypeStruct((2, rows, slots, lanes), f32)
    edge = jax.ShapeDtypeStruct((2, 2, slots, lanes), f32)
    live = (channels[0, 0, :] >= 0).astype(f32)[:, None]
    live = jnp.broadcast_to(live, (slots, lanes))
    table = jax.ShapeDtypeStruct(dipole.shape[1:], f32)
    term, low, high, passed = call(start_kernel, (field, edge, edge, table), psi_in, live, dipole[0])

    ang_one = channels[0, 0, :].astype(f32)
    ang_two = channels[0, 1, :].astype(f32)
    radius_one = (first_row + jnp.arange(rows)).astype(f32) + radius_offset
    radius_two = jnp.arange(lanes).astype(f32) + radius_offset
    potential = (
        (ang_one * (ang_one + 1.0))[None, :, None] / (radius_one**2)[:, None, None]
        + (ang_two * (ang_two + 1.0))[None, :, None] / (radius_two**2)[None, None, :]
        - coulomb_charge * (1.0 / radius_one[:, None, None] + 1.0 / radius_two[None, None, :])
    ) - kinetic_scale * 2.0 * center_weight
    ratio = jnp.minimum(radius_one[:, None], radius_two[None, :]) / jnp.maximum(
        radius_one[:, None], radius_two[None, :]
    )
    weight_one = jnp.broadcast_to((radius_one / (total_rows + radius_offset))[:, None], (rows, lanes))
    weight_two = jnp.broadcast_to((radius_two / (lanes + radius_offset))[None, :], (rows, lanes))

    def coefficients(small):
        small = jnp.broadcast_to(small.astype(f32), (rows, lanes))
        spare = [jnp.zeros_like(ratio)] * 3
        return jnp.stack([ratio, weight_one, weight_two, small, 1.0 - small] + spare, axis=1)

    alive = jnp.sum(channels[0, 0, :] >= 0).astype(f32)
    counts = lax.all_to_all(jnp.full((blocks, 8, 128), alive), "lgroup", 0, 0)[:, 0, 0]

    coupling = 0.5 * (multipole[0] + jnp.swapaxes(multipole[0], -1, -2))
    own = split_weights(coupling.reshape(-1, slots))
    lower = lax.ppermute(passed, "lgroup", shifts(blocks, 1))
    upward = dipole[0].reshape(-1, slots)
    downward = jnp.swapaxes(lower, -1, -2).reshape(-1, slots)
    chip_weights = split_weights(jnp.where(even, upward, downward))
    cross_weights = split_weights(jnp.where(even, downward, upward))
    onward = jnp.swapaxes(dipole[0], -1, -2).reshape(-1, slots)
    sent_weights = split_weights(jnp.where(even, lower.reshape(-1, slots), onward))

    def apply(order_index, roles, kept, state):
        term, total, low, high = state
        first = order_index == 1
        message = jax.ShapeDtypeStruct((2, rows, kept, lanes), f32)
        if first:
            copied, message = term, term
        else:
            part, copied, message = call(
                functools.partial(own_kernel, True),
                (field, field, message), term, own, roles, potential, sent_weights,
            )
        across = lax.ppermute(message, "lgroup", swaps(blocks, 1))
        beside = lax.ppermute(copied, "lgroup", swaps(blocks, 0))
        below = lax.ppermute(high, "row", shifts(strips, 1))
        above = lax.ppermute(low, "row", shifts(strips, -1))
        if first:
            part = call(functools.partial(own_kernel, False), field, term, own, roles, potential)
        last = order_index == ORDER
        outs = jax.ShapeDtypeStruct(psi_in.shape, f32) if last else (field, field, edge, edge)
        return call(
            functools.partial(finish_kernel, order_index, last),
            outs, part, across, beside, below, above, cross_weights, chip_weights, roles, live, total,
        )

    def rest(kept):
        def run(roles, state):
            for order_index in range(2, ORDER + 1):
                state = apply(order_index, roles, kept, state)
            return state

        return run

    state = apply(1, coefficients(jnp.bool_(False)), slots, (term, term, low, high))

    most = jnp.max(jnp.minimum(counts[1 : blocks - 1 : 2], counts[2:blocks:2])).astype(jnp.int32)
    place = lax.axis_index("lgroup")
    facing = jnp.clip(jnp.where(even, place - 1, place + 1), 0, blocks - 1)
    theirs = jnp.sum(jnp.where(jnp.arange(blocks) == facing, counts, 0.0))
    fewer = jnp.where(even, alive < theirs, alive <= theirs)
    sizes = list(range(24, slots, 8)) + [slots]
    chosen = jnp.sum(most > jnp.asarray(sizes[:-1], jnp.int32)).astype(jnp.int32)
    return lax.switch(chosen, [rest(kept) for kept in sizes], coefficients(fewer), state)


def solution(mesh):
    placed = (
        P(None, "lgroup", "row", None),
        P("lgroup", None, None),
        P("lgroup", None, None, None),
        P("lgroup", None, None, None),
    )
    return jax.shard_map(
        local, mesh=mesh, in_specs=placed, out_specs=P(None, "lgroup", "row", None), check_vma=False
    )
```

```python
import functools

import jax
import jax.numpy as jnp
from jax import lax
from jax.experimental import pallas as pl
from jax.experimental.pallas import tpu as pltpu
from jax.sharding import PartitionSpec as P

ORDER = 4

kinetic_scale = 0.2
coulomb_charge = 4.0
radius_offset = 16.0
center_weight = -2.5
near_weight = 4.0 / 3.0
far_weight = -1.0 / 12.0

near = -kinetic_scale * near_weight
far = -kinetic_scale * far_weight

f32 = jnp.float32
bf16 = jnp.bfloat16


def split_weights(mat):
    rounded = lax.reduce_precision(mat, 8, 7)
    high = rounded.astype(bf16)
    low = (mat - rounded).astype(bf16)
    return jnp.concatenate([high, high, low], axis=1)


def split_field(x):
    high = x.astype(bf16)
    low = (x - high.astype(f32)).astype(bf16)
    return jnp.concatenate([high, low, high], axis=0)


def both(ref, i):
    if len(ref.shape) == 3:
        return jnp.concatenate([ref[i], ref[ref.shape[0] // 2 + i]], axis=1)
    return jnp.concatenate([ref[0, i], ref[1, i]], axis=1)


def times(weights, x):
    return jnp.dot(weights, split_field(x), preferred_element_type=f32)


def twice(row):
    return jnp.concatenate([row, row], axis=1)


def start_kernel(psi_ref, live_ref, dipole_ref, term_ref, low_ref, high_ref, packed_ref):
    live = live_ref[...]
    rows = term_ref.shape[1]
    for s in range(2):
        for i in range(rows):
            value = psi_ref[s, :, i, :] * live
            term_ref[s, i] = value
            packed_ref[s * rows + i] = value
    low_ref[...] = term_ref[:, 0:2]
    high_ref[...] = term_ref[:, rows - 2 : rows]
    packed_ref[2 * rows] = jnp.concatenate([dipole_ref[0], dipole_ref[1]], axis=1)


def weights_kernel(across_ref, beside_ref, dipole_ref, even_ref, chip_ref, cross_ref, sent_ref):
    slots = dipole_ref.shape[1]
    plane = across_ref.shape[0] - 1
    even = even_ref[...] > 0.5
    for d in range(2):
        columns = slice(d * slots, (d + 1) * slots)
        lower = jnp.where(even, across_ref[plane][:, columns], beside_ref[plane][:, columns])
        upward = dipole_ref[d]
        downward = lower.T
        for ref, mat in (
            (chip_ref, jnp.where(even, upward, downward)),
            (cross_ref, jnp.where(even, downward, upward)),
            (sent_ref, jnp.where(even, lower, upward.T)),
        ):
            high = mat.astype(bf16).astype(f32)
            ref[columns] = jnp.concatenate([high, high, mat - high], axis=1).astype(bf16)


def own_kernel(sends, term_ref, weights_ref, coef_ref, pot_ref, *refs):
    if sends:
        sent_ref, out_ref, copy_ref, message_ref = refs
        copy_ref[...] = term_ref[...]
        kept = message_ref.shape[2]
    else:
        (out_ref,) = refs
    rows, slots, lanes = term_ref.shape[1:]
    lane = lax.broadcasted_iota(jnp.int32, (slots, lanes), 1)
    weights = weights_ref[...]
    for i in range(rows):
        here = both(term_ref, i)
        if sends:
            sent = times(sent_ref[...], here)
            sent = twice(coef_ref[i, 1:2]) * sent[:kept] + twice(coef_ref[i, 2:3]) * sent[slots : slots + kept]
            sent = twice(coef_ref[i, 3:4]) * here[:kept] + twice(coef_ref[i, 4:5]) * sent
            for s in range(2):
                message_ref[s, i] = sent[:, s * lanes : (s + 1) * lanes]
        mixed = times(weights, here)
        ratio = twice(coef_ref[i, 0:1])
        mixed = mixed[:slots] + ratio * (mixed[slots : 2 * slots] + ratio * mixed[2 * slots :])
        for s in range(2):
            x = term_ref[s, i]
            acc = mixed[:, s * lanes : (s + 1) * lanes] + pot_ref[i] * x
            close = jnp.where(lane >= 1, pltpu.roll(x, 1, 1), 0.0) + jnp.where(
                lane < lanes - 1, pltpu.roll(x, lanes - 1, 1), 0.0
            )
            wide = jnp.where(lane >= 2, pltpu.roll(x, 2, 1), 0.0) + jnp.where(
                lane < lanes - 2, pltpu.roll(x, lanes - 2, 1), 0.0
            )
            for step in (-1, 1):
                if 0 <= i + step < rows:
                    close = close + term_ref[s, i + step]
                if 0 <= i + 2 * step < rows:
                    wide = wide + term_ref[s, i + 2 * step]
            out_ref[s, i] = acc + near * close + far * wide


def finish_kernel(
    order_index, last, part_ref, across_ref, beside_ref, below_ref, above_ref,
    cross_ref, chip_ref, coef_ref, live_ref, total_ref, *outs
):
    rows, slots, lanes = part_ref.shape[1:]
    kept = across_ref.shape[-2]
    scale = live_ref[...] / float(order_index)
    for i in range(rows):
        came = both(across_ref, i)
        if kept < slots:
            came = jnp.concatenate([came, jnp.zeros((slots - kept, 2 * lanes), f32)], axis=0)
        raw = came * twice(coef_ref[i, 4:5])
        mixed = times(cross_ref[...], raw) + times(chip_ref[...], both(beside_ref, i))
        mixed = twice(coef_ref[i, 1:2]) * mixed[:slots] + twice(coef_ref[i, 2:3]) * mixed[slots:]
        mixed = mixed + came * twice(coef_ref[i, 3:4])
        image = []
        for s in range(2):
            acc = part_ref[s, i] + mixed[:, s * lanes : (s + 1) * lanes]
            if i == 0:
                acc = acc + near * below_ref[s, 1] + far * below_ref[s, 0]
            if i == 1:
                acc = acc + far * below_ref[s, 1]
            if i == rows - 1:
                acc = acc + near * above_ref[s, 0] + far * above_ref[s, 1]
            if i == rows - 2:
                acc = acc + far * above_ref[s, 0]
            image.append(acc * scale)
        real, imag = image[1], -image[0]
        if last:
            outs[0][0, :, i, :] = total_ref[0, i] + real
            outs[0][1, :, i, :] = total_ref[1, i] + imag
            continue
        for s, value in enumerate((real, imag)):
            outs[0][s, i] = value
            outs[1][s, i] = total_ref[s, i] + value
            if i < 2:
                outs[2][s, i] = value
            if i >= rows - 2:
                outs[3][s, i - (rows - 2)] = value


def call(kernel, outs, *args):
    cost = pl.CostEstimate(flops=800_000_000, bytes_accessed=3_000_000, transcendentals=0)
    return pl.pallas_call(
        kernel,
        out_shape=outs,
        cost_estimate=cost,
        compiler_params=pltpu.CompilerParams(vmem_limit_bytes=32 * 1024 * 1024),
    )(*args)


def swaps(count, first):
    found = []
    for i in range(first, count - 1, 2):
        found += [(i, i + 1), (i + 1, i)]
    return found


def shifts(count, by):
    return [(i, i + by) for i in range(count) if 0 <= i + by < count]


def local(psi_in, channels, multipole, dipole):
    _, slots, rows, lanes = psi_in.shape
    blocks = lax.axis_size("lgroup")
    strips = lax.axis_size("row")
    total_rows = strips * rows
    first_row = lax.axis_index("row") * rows
    even = lax.axis_index("lgroup") % 2 == 0

    field = jax.ShapeDtypeStruct((2, rows, slots, lanes), f32)
    edge = jax.ShapeDtypeStruct((2, 2, slots, lanes), f32)
    live = (channels[0, 0, :] >= 0).astype(f32)[:, None]
    live = jnp.broadcast_to(live, (slots, lanes))
    packing = jax.ShapeDtypeStruct((2 * rows + 1, slots, lanes), f32)
    term, low, high, packed = call(start_kernel, (field, edge, edge, packing), psi_in, live, dipole[0])

    ang_one = channels[0, 0, :].astype(f32)
    ang_two = channels[0, 1, :].astype(f32)
    radius_one = (first_row + jnp.arange(rows)).astype(f32) + radius_offset
    radius_two = jnp.arange(lanes).astype(f32) + radius_offset
    potential = (
        (ang_one * (ang_one + 1.0))[None, :, None] / (radius_one**2)[:, None, None]
        + (ang_two * (ang_two + 1.0))[None, :, None] / (radius_two**2)[None, None, :]
        - coulomb_charge * (1.0 / radius_one[:, None, None] + 1.0 / radius_two[None, None, :])
    ) - kinetic_scale * 2.0 * center_weight
    ratio = jnp.minimum(radius_one[:, None], radius_two[None, :]) / jnp.maximum(
        radius_one[:, None], radius_two[None, :]
    )
    weight_one = jnp.broadcast_to((radius_one / (total_rows + radius_offset))[:, None], (rows, lanes))
    weight_two = jnp.broadcast_to((radius_two / (lanes + radius_offset))[None, :], (rows, lanes))

    def coefficients(small):
        small = jnp.broadcast_to(small.astype(f32), (rows, lanes))
        spare = [jnp.zeros_like(ratio)] * 3
        return jnp.stack([ratio, weight_one, weight_two, small, 1.0 - small] + spare, axis=1)

    alive = jnp.sum(channels[0, 0, :] >= 0).astype(f32)
    counts = lax.all_to_all(jnp.full((blocks, 8, 128), alive), "lgroup", 0, 0)[:, 0, 0]

    coupling = 0.5 * (multipole[0] + jnp.swapaxes(multipole[0], -1, -2))
    own = split_weights(coupling.reshape(-1, slots))
    def apply(order_index, roles, kept, state, matrices=None):
        term, total, low, high = state
        first = order_index == 1
        message = jax.ShapeDtypeStruct((2, rows, kept, lanes), f32)
        if first:
            copied, message = packed, packed
        else:
            part, copied, message = call(
                functools.partial(own_kernel, True),
                (field, field, message), term, own, roles, potential, matrices[2],
            )
        across = lax.ppermute(message, "lgroup", swaps(blocks, 1))
        beside = lax.ppermute(copied, "lgroup", swaps(blocks, 0))
        below = lax.ppermute(high, "row", shifts(strips, 1))
        above = lax.ppermute(low, "row", shifts(strips, -1))
        if first:
            part = call(functools.partial(own_kernel, False), field, term, own, roles, potential)
            parity = jnp.broadcast_to(even.astype(f32), (slots, slots))
            split = jax.ShapeDtypeStruct((2 * slots, 3 * slots), bf16)
            matrices = call(weights_kernel, (split, split, split), across, beside, dipole[0], parity)
        last = order_index == ORDER
        outs = jax.ShapeDtypeStruct(psi_in.shape, f32) if last else (field, field, edge, edge)
        done = call(
            functools.partial(finish_kernel, order_index, last),
            outs, part, across, beside, below, above, matrices[1], matrices[0], roles, live, total,
        )
        return (done, matrices) if first else done

    def rest(kept):
        def run(roles, state, matrices):
            for order_index in range(2, ORDER + 1):
                state = apply(order_index, roles, kept, state, matrices)
            return state

        return run

    state, matrices = apply(1, coefficients(jnp.bool_(False)), slots, (term, term, low, high))

    most = jnp.max(jnp.minimum(counts[1 : blocks - 1 : 2], counts[2:blocks:2])).astype(jnp.int32)
    place = lax.axis_index("lgroup")
    facing = jnp.clip(jnp.where(even, place - 1, place + 1), 0, blocks - 1)
    theirs = jnp.sum(jnp.where(jnp.arange(blocks) == facing, counts, 0.0))
    fewer = jnp.where(even, alive < theirs, alive <= theirs)
    sizes = list(range(24, slots, 8)) + [slots]
    chosen = jnp.sum(most > jnp.asarray(sizes[:-1], jnp.int32)).astype(jnp.int32)
    return lax.switch(chosen, [rest(kept) for kept in sizes], coefficients(fewer), state, matrices)


def solution(mesh):
    placed = (
        P(None, "lgroup", "row", None),
        P("lgroup", None, None),
        P("lgroup", None, None, None),
        P("lgroup", None, None, None),
    )
    return jax.shard_map(
        local, mesh=mesh, in_specs=placed, out_specs=P(None, "lgroup", "row", None), check_vma=False
    )
```

```python
import functools

import jax
import jax.numpy as jnp
from jax import lax
from jax.experimental import pallas as pl
from jax.experimental.pallas import tpu as pltpu
from jax.sharding import PartitionSpec as P

ORDER = 4

kinetic_scale = 0.2
coulomb_charge = 4.0
radius_offset = 16.0
center_weight = -2.5
near_weight = 4.0 / 3.0
far_weight = -1.0 / 12.0

near = -kinetic_scale * near_weight
far = -kinetic_scale * far_weight

f32 = jnp.float32
bf16 = jnp.bfloat16


def split_weights(mat):
    rounded = lax.reduce_precision(mat, 8, 7)
    high = rounded.astype(bf16)
    low = (mat - rounded).astype(bf16)
    return jnp.concatenate([high, high, low], axis=1)


def split_field(x):
    high = x.astype(bf16)
    low = (x - high.astype(f32)).astype(bf16)
    return jnp.concatenate([high, low, high], axis=0)


def both(ref, i):
    return jnp.concatenate([ref[0, i], ref[1, i]], axis=1)


def times(weights, x):
    return jnp.dot(weights, split_field(x), preferred_element_type=f32)


def twice(row):
    return jnp.concatenate([row, row], axis=1)


def start_kernel(psi_ref, live_ref, dipole_ref, term_ref, low_ref, high_ref, sent_ref):
    sent_ref[...] = dipole_ref[...]
    live = live_ref[...]
    rows = term_ref.shape[1]
    for s in range(2):
        for i in range(rows):
            term_ref[s, i] = psi_ref[s, :, i, :] * live
    low_ref[...] = term_ref[:, 0:2]
    high_ref[...] = term_ref[:, rows - 2 : rows]


def own_kernel(sends, term_ref, weights_ref, coef_ref, pot_ref, *refs):
    if sends:
        sent_ref, out_ref, message_ref = refs
        kept = message_ref.shape[2]
    else:
        (out_ref,) = refs
    rows, slots, lanes = term_ref.shape[1:]
    lane = lax.broadcasted_iota(jnp.int32, (slots, lanes), 1)
    weights = weights_ref[...]
    for i in range(rows):
        here = both(term_ref, i)
        if sends:
            sent = times(sent_ref[...], here)
            sent = twice(coef_ref[i, 1:2]) * sent[:kept] + twice(coef_ref[i, 2:3]) * sent[slots : slots + kept]
            sent = twice(coef_ref[i, 3:4]) * here[:kept] + twice(coef_ref[i, 4:5]) * sent
            for s in range(2):
                message_ref[s, i] = sent[:, s * lanes : (s + 1) * lanes]
        mixed = times(weights, here)
        ratio = twice(coef_ref[i, 0:1])
        mixed = mixed[:slots] + ratio * (mixed[slots : 2 * slots] + ratio * mixed[2 * slots :])
        for s in range(2):
            x = term_ref[s, i]
            acc = mixed[:, s * lanes : (s + 1) * lanes] + pot_ref[i] * x
            close = jnp.where(lane >= 1, pltpu.roll(x, 1, 1), 0.0) + jnp.where(
                lane < lanes - 1, pltpu.roll(x, lanes - 1, 1), 0.0
            )
            wide = jnp.where(lane >= 2, pltpu.roll(x, 2, 1), 0.0) + jnp.where(
                lane < lanes - 2, pltpu.roll(x, lanes - 2, 1), 0.0
            )
            for step in (-1, 1):
                if 0 <= i + step < rows:
                    close = close + term_ref[s, i + step]
                if 0 <= i + 2 * step < rows:
                    wide = wide + term_ref[s, i + 2 * step]
            out_ref[s, i] = acc + near * close + far * wide


def finish_kernel(
    order_index, last, part_ref, across_ref, beside_ref, below_ref, above_ref,
    cross_ref, chip_ref, coef_ref, live_ref, total_ref, *outs
):
    rows, slots, lanes = part_ref.shape[1:]
    kept = across_ref.shape[2]
    scale = live_ref[...] / float(order_index)
    for i in range(rows):
        came = both(across_ref, i)
        if kept < slots:
            came = jnp.concatenate([came, jnp.zeros((slots - kept, 2 * lanes), f32)], axis=0)
        raw = came * twice(coef_ref[i, 4:5])
        mixed = times(cross_ref[...], raw) + times(chip_ref[...], both(beside_ref, i))
        mixed = twice(coef_ref[i, 1:2]) * mixed[:slots] + twice(coef_ref[i, 2:3]) * mixed[slots:]
        mixed = mixed + came * twice(coef_ref[i, 3:4])
        image = []
        for s in range(2):
            acc = part_ref[s, i] + mixed[:, s * lanes : (s + 1) * lanes]
            if i == 0:
                acc = acc + near * below_ref[s, 1] + far * below_ref[s, 0]
            if i == 1:
                acc = acc + far * below_ref[s, 1]
            if i == rows - 1:
                acc = acc + near * above_ref[s, 0] + far * above_ref[s, 1]
            if i == rows - 2:
                acc = acc + far * above_ref[s, 0]
            image.append(acc * scale)
        real, imag = image[1], -image[0]
        if last:
            outs[0][0, :, i, :] = total_ref[0, i] + real
            outs[0][1, :, i, :] = total_ref[1, i] + imag
            continue
        for s, value in enumerate((real, imag)):
            outs[0][s, i] = value
            outs[1][s, i] = total_ref[s, i] + value
            if i < 2:
                outs[2][s, i] = value
            if i >= rows - 2:
                outs[3][s, i - (rows - 2)] = value


def call(kernel, outs, *args):
    cost = pl.CostEstimate(flops=800_000_000, bytes_accessed=3_000_000, transcendentals=0)
    return pl.pallas_call(
        kernel,
        out_shape=outs,
        cost_estimate=cost,
        compiler_params=pltpu.CompilerParams(vmem_limit_bytes=32 * 1024 * 1024),
    )(*args)


def swaps(count, first):
    found = []
    for i in range(first, count - 1, 2):
        found += [(i, i + 1), (i + 1, i)]
    return found


def shifts(count, by):
    return [(i, i + by) for i in range(count) if 0 <= i + by < count]


def local(psi_in, channels, multipole, dipole):
    _, slots, rows, lanes = psi_in.shape
    blocks = lax.axis_size("lgroup")
    strips = lax.axis_size("row")
    total_rows = strips * rows
    first_row = lax.axis_index("row") * rows
    even = lax.axis_index("lgroup") % 2 == 0

    field = jax.ShapeDtypeStruct((2, rows, slots, lanes), f32)
    edge = jax.ShapeDtypeStruct((2, 2, slots, lanes), f32)
    live = (channels[0, 0, :] >= 0).astype(f32)[:, None]
    live = jnp.broadcast_to(live, (slots, lanes))
    table = jax.ShapeDtypeStruct(dipole.shape[1:], f32)
    term, low, high, passed = call(start_kernel, (field, edge, edge, table), psi_in, live, dipole[0])

    ang_one = channels[0, 0, :].astype(f32)
    ang_two = channels[0, 1, :].astype(f32)
    radius_one = (first_row + jnp.arange(rows)).astype(f32) + radius_offset
    radius_two = jnp.arange(lanes).astype(f32) + radius_offset
    potential = (
        (ang_one * (ang_one + 1.0))[None, :, None] / (radius_one**2)[:, None, None]
        + (ang_two * (ang_two + 1.0))[None, :, None] / (radius_two**2)[None, None, :]
        - coulomb_charge * (1.0 / radius_one[:, None, None] + 1.0 / radius_two[None, None, :])
    ) - kinetic_scale * 2.0 * center_weight
    ratio = jnp.minimum(radius_one[:, None], radius_two[None, :]) / jnp.maximum(
        radius_one[:, None], radius_two[None, :]
    )
    weight_one = jnp.broadcast_to((radius_one / (total_rows + radius_offset))[:, None], (rows, lanes))
    weight_two = jnp.broadcast_to((radius_two / (lanes + radius_offset))[None, :], (rows, lanes))

    def coefficients(small):
        small = jnp.broadcast_to(small.astype(f32), (rows, lanes))
        spare = [jnp.zeros_like(ratio)] * 3
        return jnp.stack([ratio, weight_one, weight_two, small, 1.0 - small] + spare, axis=1)

    alive = jnp.sum(channels[0, 0, :] >= 0).astype(f32)
    counts = lax.all_to_all(jnp.full((blocks, 8, 128), alive), "lgroup", 0, 0)[:, 0, 0]

    coupling = 0.5 * (multipole[0] + jnp.swapaxes(multipole[0], -1, -2))
    own = split_weights(coupling.reshape(-1, slots))
    lower = lax.ppermute(passed, "lgroup", shifts(blocks, 1))
    upward = dipole[0].reshape(-1, slots)
    downward = jnp.swapaxes(lower, -1, -2).reshape(-1, slots)
    chip_weights = split_weights(jnp.where(even, upward, downward))
    cross_weights = split_weights(jnp.where(even, downward, upward))
    onward = jnp.swapaxes(dipole[0], -1, -2).reshape(-1, slots)
    sent_weights = split_weights(jnp.where(even, lower.reshape(-1, slots), onward))

    def apply(order_index, roles, kept, state):
        term, total, low, high = state
        first = order_index == 1
        message = jax.ShapeDtypeStruct((2, rows, kept, lanes), f32)
        if first:
            copied, message = term, term
        else:
            copied = term
            part, message = call(
                functools.partial(own_kernel, True),
                (field, message), term, own, roles, potential, sent_weights,
            )
        across = lax.ppermute(message, "lgroup", swaps(blocks, 1))
        beside = lax.ppermute(copied, "lgroup", swaps(blocks, 0))
        below = lax.ppermute(high, "row", shifts(strips, 1))
        above = lax.ppermute(low, "row", shifts(strips, -1))
        if first:
            part = call(functools.partial(own_kernel, False), field, term, own, roles, potential)
        last = order_index == ORDER
        outs = jax.ShapeDtypeStruct(psi_in.shape, f32) if last else (field, field, edge, edge)
        return call(
            functools.partial(finish_kernel, order_index, last),
            outs, part, across, beside, below, above, cross_weights, chip_weights, roles, live, total,
        )

    def rest(kept):
        def run(roles, state):
            for order_index in range(2, ORDER + 1):
                state = apply(order_index, roles, kept, state)
            return state

        return run

    state = apply(1, coefficients(jnp.bool_(False)), slots, (term, term, low, high))

    most = jnp.max(jnp.minimum(counts[1 : blocks - 1 : 2], counts[2:blocks:2])).astype(jnp.int32)
    place = lax.axis_index("lgroup")
    facing = jnp.clip(jnp.where(even, place - 1, place + 1), 0, blocks - 1)
    theirs = jnp.sum(jnp.where(jnp.arange(blocks) == facing, counts, 0.0))
    fewer = jnp.where(even, alive < theirs, alive <= theirs)
    sizes = list(range(24, slots, 8)) + [slots]
    chosen = jnp.sum(most > jnp.asarray(sizes[:-1], jnp.int32)).astype(jnp.int32)
    return lax.switch(chosen, [rest(kept) for kept in sizes], coefficients(fewer), state)


def solution(mesh):
    placed = (
        P(None, "lgroup", "row", None),
        P("lgroup", None, None),
        P("lgroup", None, None, None),
        P("lgroup", None, None, None),
    )
    return jax.shard_map(
        local, mesh=mesh, in_specs=placed, out_specs=P(None, "lgroup", "row", None), check_vma=False
    )
```
